32 devices in a mesh: dp: 4 (over y, x), feat: 2 (over core), cent: 4 (over z).
Axes of the slice: x: 2, y: 2, z: 4, core: 2. Of those that a mesh axis runs over, the one named last changes fastest.
Arguments:
- embeddings: bfloat16 [4096, 768], P(('dp', 'cent')), may hold values from -12 to 12
- projection: bfloat16 [768, 8192], P(None, 'feat'), may hold values from -0.21875 to 0.21875
- phases: float32 [8192], P('feat'), may hold values from -4 to 4
- centroids: bfloat16 [4096, 8192], P('cent', 'feat'), may hold values from -7 to 7
Outputs:
- updated: float32 [4096, 8192], P('cent', 'feat')
The draws below stay inside these ranges and needn't reach their ends.
All inputs are finite; a program needn't handle non-finite values.
Results may differ from the reference program's by a relative error of at most 0.0003.
Values may be sent and summed in bfloat16 or wider, within the bound.
A program may use at most 192 MiB of HBM per device.

```python
import math
import jax
import jax.numpy as jnp
from jax import lax

E = 768
F = 8192
K = 4096
ROWS = 4096


def phase_values(key):
    return jax.random.uniform(jax.random.fold_in(key, 17), (F,), jnp.float32, -math.pi, math.pi)


def draw_phases(key, part):
    return phase_values(key)


def draw_embeddings(key, part):
    raw_normal = jax.random.normal(jax.random.fold_in(key, 23), (ROWS, E), jnp.float32)
    values = jnp.clip(raw_normal, -6.0, 6.0)
    return values.astype(jnp.bfloat16)


def draw_centroids(key, part):
    values = jnp.clip(jax.random.normal(jax.random.fold_in(key, 29), (K, F), jnp.float32), -6.0, 6.0)
    return values.astype(jnp.bfloat16)


def block_scale(stream_key, shape, split, low, largest):
    loudness = 1.0
    for position, shards_of in split:
        heights = jax.random.uniform(jax.random.fold_in(jax.random.fold_in(stream_key, 6), position), (shards_of,), jnp.float32, low / len(split), largest / len(split))
        loudness = loudness * jnp.repeat(jnp.exp(heights), shape[position] // shards_of).reshape((-1,) + (1,) * (len(shape) - 1 - position))
    return loudness


def scatter_about(key, extent, deviation, limit, pieces=(), kind=jnp.bfloat16):
    result = jax.random.normal(key, extent, jnp.float32) * deviation
    if len(pieces) > 0:
        result = block_scale(key, extent, pieces, -0.22, 0.18) * result
    return jnp.clip(result, min=-limit, max=limit).astype(kind)


def setup_inputs(seed: int = 0) -> dict:
    arg_keys = jax.random.split(jax.random.key(seed), 5)
    embeddings = draw_embeddings(jax.random.fold_in(arg_keys[4], 71), 0)
    projection = scatter_about(arg_keys[1], (E, F), E ** -0.5, 0.21875, ((1, 2),))
    phases = draw_phases(jax.random.fold_in(arg_keys[4], 71), 0)
    centroids = draw_centroids(jax.random.fold_in(arg_keys[4], 71), 0)
    return {"embeddings": embeddings, "projection": projection, "phases": phases, "centroids": centroids}


SQRT_TWO = math.sqrt(2.0)
SHARP_FACTOR = 1.5
PRIOR_MASS = 1.0

def reference(embeddings, projection, phases, centroids):
    projected = jnp.dot(embeddings, projection, preferred_element_type=jnp.float32)
    features = (SQRT_TWO * jnp.cos(projected + phases)).astype(jnp.bfloat16)
    center_wide = centroids.astype(jnp.float32)
    center_sq = lax.optimization_barrier(jnp.sum(center_wide * center_wide, axis=1))
    inner_prod = jnp.dot(features, centroids.T, preferred_element_type=jnp.float32)
    sharpness = SHARP_FACTOR / math.sqrt(F)
    logits = sharpness * (2.0 * inner_prod - center_sq[None, :])
    top_score = lax.optimization_barrier(jnp.max(logits, axis=1, keepdims=True))
    exp_terms = jnp.exp(logits - top_score)
    resp = (exp_terms / lax.optimization_barrier(jnp.sum(exp_terms, axis=1, keepdims=True))).astype(jnp.bfloat16)
    mass = lax.optimization_barrier(jnp.sum(resp.astype(jnp.float32), axis=0))
    sums = jnp.dot(resp.T, features, preferred_element_type=jnp.float32)
    return (sums + PRIOR_MASS * center_wide) / (mass + PRIOR_MASS)[:, None]
```

```python
import functools
import math

import jax
import jax.numpy as jnp
from jax import lax
from jax.experimental import pallas as pl
from jax.experimental.pallas import tpu as pltpu
from jax.sharding import PartitionSpec as P

F = 8192
SHARP_FACTOR = 1.5
PRIOR_MASS = 1.0

COS_COEFS = (
    1.4142135468471868,
    -0.7071066266011933,
    0.058925313538275806,
    -0.0019640317236862027,
    3.502984094725661e-05,
    -3.829489560381237e-07,
    2.4385896105334273e-09,
)
INV_TURN = 1.0 / (2.0 * math.pi)
TURN_HI = 6.28125
TURN_LO = 2.0 * math.pi - TURN_HI


def scaled_cos(x):
    turns = jnp.round(x * INV_TURN)
    r = (x - turns * TURN_HI) - turns * TURN_LO
    u = r * r
    y = COS_COEFS[-1]
    for c in COS_COEFS[-2::-1]:
        y = y * u + c
    return y


def feature_kernel(sub_rows, sub_cols, e_ref, p_ref, b_ref, o_ref):
    rows, cols = o_ref.shape
    for j in range(cols // sub_cols):
        cs = slice(j * sub_cols, (j + 1) * sub_cols)
        for i in range(rows // sub_rows):
            rs = slice(i * sub_rows, (i + 1) * sub_rows)
            x = jnp.dot(e_ref[rs, :], p_ref[:, cs], preferred_element_type=jnp.float32)
            o_ref[rs, cs] = scaled_cos(x + b_ref[:, cs]).astype(jnp.bfloat16)


def featurize(embeddings, projection, phases):
    rows, width = embeddings.shape
    cols = projection.shape[1]
    tr, tc = min(512, rows), min(1024, cols)
    return pl.pallas_call(
        functools.partial(feature_kernel, min(256, tr), min(256, tc)),
        grid=(cols // tc, rows // tr),
        in_specs=[
            pl.BlockSpec((tr, width), lambda j, i: (i, 0)),
            pl.BlockSpec((width, tc), lambda j, i: (0, j)),
            pl.BlockSpec((1, tc), lambda j, i: (0, j)),
        ],
        out_specs=pl.BlockSpec((tr, tc), lambda j, i: (i, j)),
        out_shape=jax.ShapeDtypeStruct((rows, cols), jnp.bfloat16),
        compiler_params=pltpu.CompilerParams(vmem_limit_bytes=32 << 20),
        cost_estimate=pl.CostEstimate(
            flops=2 * rows * width * cols,
            bytes_accessed=2 * (rows * cols + rows * width + width * cols),
            transcendentals=rows * cols,
        ),
        name="featurize",
    )(embeddings, projection, phases.reshape(1, cols))


def sums_kernel(r_ref, f_ref, c_ref, m_ref, o_ref):
    groups, _, depth = r_ref.shape
    total = None
    for g in range(groups):
        part = jnp.dot(
            r_ref[g],
            f_ref[g * depth : (g + 1) * depth, :],
            preferred_element_type=jnp.float32,
        )
        total = part if total is None else total + part
    o_ref[...] = (total + PRIOR_MASS * c_ref[...].astype(jnp.float32)) / (
        m_ref[...] + PRIOR_MASS
    )


def update(resp, features, centroids, mass):
    groups, cents, depth = resp.shape
    rows, cols = features.shape
    tk, tc = min(512, cents), min(512, cols)
    return pl.pallas_call(
        sums_kernel,
        grid=(cents // tk, cols // tc),
        in_specs=[
            pl.BlockSpec((groups, tk, depth), lambda i, j: (0, i, 0)),
            pl.BlockSpec((rows, tc), lambda i, j: (0, j)),
            pl.BlockSpec((tk, tc), lambda i, j: (i, j)),
            pl.BlockSpec((tk, 1), lambda i, j: (i, 0)),
        ],
        out_specs=pl.BlockSpec((tk, tc), lambda i, j: (i, j)),
        out_shape=jax.ShapeDtypeStruct((cents, cols), jnp.float32),
        compiler_params=pltpu.CompilerParams(vmem_limit_bytes=48 << 20),
        cost_estimate=pl.CostEstimate(
            flops=2 * rows * cents * cols,
            bytes_accessed=2 * (rows * cols + rows * cents) + 6 * cents * cols,
            transcendentals=0,
        ),
        name="update",
    )(resp, features, centroids, mass)


def my_part(x, axis_name):
    size = x.shape[0] // lax.axis_size(axis_name)
    return lax.dynamic_slice_in_dim(x, lax.axis_index(axis_name) * size, size, 0)


def shards(embeddings, projection, phases, centroids):
    sharpness = SHARP_FACTOR / math.sqrt(F)
    own = lax.all_gather(my_part(embeddings, "feat"), ("cent", "feat"), axis=0, tiled=True)
    every = lax.all_gather(my_part(own, "feat"), ("dp", "feat"), axis=0, tiled=True)
    wide = centroids.astype(jnp.float32)
    center_sq = jnp.sum(wide * wide, axis=1)
    own_features = featurize(own, projection, phases)
    inner = lax.dot_general(
        centroids, own_features, (((1,), (1,)), ((), ())), preferred_element_type=jnp.float32
    )
    partial_value = 2.0 * inner - center_sq[:, None]
    logits = sharpness * lax.psum_scatter(
        partial_value, "feat", scatter_dimension=1, tiled=True
    )
    top = jnp.max(logits, axis=0)
    local_sum = jnp.sum(jnp.exp(logits - top[None, :]), axis=0)
    stats = lax.all_gather(jnp.stack([top, local_sum]), "cent", axis=0, tiled=False)
    peak = jnp.max(stats[:, 0], axis=0)
    norm = jnp.sum(stats[:, 1] * jnp.exp(stats[:, 0] - peak[None, :]), axis=0)
    resp = (jnp.exp(logits - peak[None, :]) / norm[None, :]).astype(jnp.bfloat16)
    all_resp = lax.all_gather(resp, ("dp", "feat"), axis=0, tiled=False)
    features = featurize(every, projection, phases)
    mass = jnp.sum(all_resp.astype(jnp.float32), axis=(0, 2))
    return update(all_resp, features, centroids, mass[:, None])


def solution(mesh):
    return jax.shard_map(
        shards,
        mesh=mesh,
        in_specs=(P(("dp", "cent"), None), P(None, "feat"), P("feat"), P("cent", "feat")),
        out_specs=P("cent", "feat"),
        check_vma=False,
    )
```

```python
import functools
import math

import jax
import jax.numpy as jnp
from jax import lax
from jax.experimental import pallas as pl
from jax.experimental.pallas import tpu as pltpu
from jax.sharding import PartitionSpec as P

F = 8192
SHARP_FACTOR = 1.5
PRIOR_MASS = 1.0

COS_COEFS = (
    1.4142135468471868,
    -0.7071066266011933,
    0.058925313538275806,
    -0.0019640317236862027,
    3.502984094725661e-05,
    -3.829489560381237e-07,
    2.4385896105334273e-09,
)
INV_TURN = 1.0 / (2.0 * math.pi)
TURN_COEFS = tuple(c * (2.0 * math.pi) ** (2 * k) for k, c in enumerate(COS_COEFS))


def scaled_cos(x):
    turns = x * INV_TURN
    r = turns - jnp.round(turns)
    u = r * r
    y = TURN_COEFS[-1]
    for c in TURN_COEFS[-2::-1]:
        y = y * u + c
    return y


def feature_kernel(sub_rows, sub_cols, e_ref, p_ref, b_ref, o_ref):
    rows, cols = o_ref.shape
    held = None
    for j in range(cols // sub_cols):
        cs = slice(j * sub_cols, (j + 1) * sub_cols)
        for i in range(rows // sub_rows):
            rs = slice(i * sub_rows, (i + 1) * sub_rows)
            x = jnp.dot(e_ref[rs, :], p_ref[:, cs], preferred_element_type=jnp.float32)
            if held is not None:
                hr, hc, hx = held
                o_ref[hr, hc] = scaled_cos(hx + b_ref[:, hc]).astype(jnp.bfloat16)
            held = rs, cs, x
    hr, hc, hx = held
    o_ref[hr, hc] = scaled_cos(hx + b_ref[:, hc]).astype(jnp.bfloat16)


def featurize(embeddings, projection, phases):
    rows, width = embeddings.shape
    cols = projection.shape[1]
    tr, tc = min(1024, rows), min(1024, cols)
    return pl.pallas_call(
        functools.partial(feature_kernel, min(128, tr), min(256, tc)),
        grid=(cols // tc, rows // tr),
        in_specs=[
            pl.BlockSpec((tr, width), lambda j, i: (i, 0)),
            pl.BlockSpec((width, tc), lambda j, i: (0, j)),
            pl.BlockSpec((1, tc), lambda j, i: (0, j)),
        ],
        out_specs=pl.BlockSpec((tr, tc), lambda j, i: (i, j)),
        out_shape=jax.ShapeDtypeStruct((rows, cols), jnp.bfloat16),
        compiler_params=pltpu.CompilerParams(vmem_limit_bytes=32 << 20),
        cost_estimate=pl.CostEstimate(
            flops=6 * rows * width * cols,
            bytes_accessed=2 * (rows * cols + rows * width + width * cols),
            transcendentals=0,
        ),
        name="featurize",
    )(embeddings, projection, phases.reshape(1, cols))


def score_kernel(tile, c_ref, f_ref, s_ref, o_ref):
    cents = c_ref.shape[0]
    for i in range(cents // tile):
        rs = slice(i * tile, (i + 1) * tile)
        inner = lax.dot_general(
            c_ref[rs, :],
            f_ref[...],
            (((1,), (1,)), ((), ())),
            preferred_element_type=jnp.float32,
        )
        o_ref[0, rs, :] = 2.0 * inner - s_ref[rs, :]


def score(centroids, features, center_sq, groups):
    cents, cols = centroids.shape
    rows = features.shape[0]
    size = rows // groups
    return pl.pallas_call(
        functools.partial(score_kernel, min(256, cents)),
        grid=(groups,),
        in_specs=[
            pl.BlockSpec((cents, cols), lambda g: (0, 0)),
            pl.BlockSpec((size, cols), lambda g: (g, 0)),
            pl.BlockSpec((cents, 1), lambda g: (0, 0)),
        ],
        out_specs=pl.BlockSpec((1, cents, size), lambda g: (g, 0, 0)),
        out_shape=jax.ShapeDtypeStruct((groups, cents, size), jnp.float32),
        compiler_params=pltpu.CompilerParams(vmem_limit_bytes=40 << 20),
        cost_estimate=pl.CostEstimate(
            flops=2 * rows * cents * cols,
            bytes_accessed=2 * (rows * cols + cents * cols) + 4 * rows * cents,
            transcendentals=0,
        ),
        name="score",
    )(centroids, features, center_sq)


def update_kernel(n_data, n_feat, i_ref, r_ref, c_ref, *refs):
    f_refs, (o_ref, k_ref, m_ref) = refs[:n_data], refs[n_data:]
    size = r_ref.shape[2]

    @pl.when(pl.program_id(0) == 0)
    def _():
        mass = jnp.zeros(m_ref.shape, jnp.float32)
        for g in range(n_data * n_feat):
            part = r_ref[i_ref[g]]
            k_ref[:, g * size : (g + 1) * size] = part
            mass += jnp.sum(part.astype(jnp.float32), axis=1, keepdims=True)
        m_ref[...] = mass

    total = PRIOR_MASS * c_ref[...].astype(jnp.float32)
    depth = n_feat * size
    for s in range(n_data):
        total += jnp.dot(
            k_ref[:, s * depth : (s + 1) * depth],
            f_refs[s][...],
            preferred_element_type=jnp.float32,
        )
    o_ref[...] = total / (m_ref[...] + PRIOR_MASS)


def update(order, resp, centroids, features, n_feat):
    groups, cents, size = resp.shape
    n_data = len(features)
    depth, cols = features[0].shape
    rows = n_data * depth
    tc = min(512, cols)
    return pl.pallas_call(
        functools.partial(update_kernel, n_data, n_feat),
        grid=(cols // tc,),
        in_specs=[
            pl.BlockSpec(memory_space=pltpu.SMEM),
            pl.BlockSpec(
                (groups, cents, size), lambda j: (0, 0, 0), pipeline_mode=pl.Buffered(1)
            ),
            pl.BlockSpec((cents, tc), lambda j: (0, j)),
        ]
        + [pl.BlockSpec((depth, tc), lambda j: (0, j))] * n_data,
        out_specs=pl.BlockSpec((cents, tc), lambda j: (0, j)),
        out_shape=jax.ShapeDtypeStruct((cents, cols), jnp.float32),
        scratch_shapes=[
            pltpu.VMEM((cents, rows), jnp.bfloat16),
            pltpu.VMEM((cents, 1), jnp.float32),
        ],
        compiler_params=pltpu.CompilerParams(vmem_limit_bytes=52 << 20),
        cost_estimate=pl.CostEstimate(
            flops=2 * rows * cents * cols,
            bytes_accessed=2 * (rows * cols + rows * cents) + 6 * cents * cols,
            transcendentals=0,
        ),
        name="update",
    )(order, resp, centroids, *features)


def my_part(x, axis_name):
    size = x.shape[0] // lax.axis_size(axis_name)
    return lax.dynamic_slice_in_dim(x, lax.axis_index(axis_name) * size, size, 0)


def from_others(x, axis_name):
    n = lax.axis_size(axis_name)
    return [
        lax.ppermute(x, axis_name, [(i, (i + s) % n) for i in range(n)]) for s in range(1, n)
    ]


def shards(embeddings, projection, phases, centroids):
    sharpness = SHARP_FACTOR / math.sqrt(F)
    n_data, n_feat = lax.axis_size("dp"), lax.axis_size("feat")
    dp, feat = lax.axis_index("dp"), lax.axis_index("feat")
    own = lax.all_gather(my_part(embeddings, "feat"), ("cent", "feat"), axis=0, tiled=True)
    halves = from_others(my_part(own, "feat"), "dp")
    wide = centroids.astype(jnp.float32)
    center_sq = jnp.sum(wide * wide, axis=1, keepdims=True)
    own_features = featurize(own, projection, phases)
    partial_value = score(centroids, own_features, center_sq, n_feat)
    partial_value, *halves = lax.optimization_barrier((partial_value, *halves))
    others = [
        jnp.concatenate([half] + from_others(half, "feat"), axis=0) for half in halves
    ]
    whole_value = lax.psum_scatter(partial_value, "feat", scatter_dimension=0)
    whole_value, *others = lax.optimization_barrier((whole_value, *others))
    logits = sharpness * whole_value
    top = jnp.max(logits, axis=0)
    local_sum = jnp.sum(jnp.exp(logits - top[None, :]), axis=0)
    stats = jnp.stack([top, local_sum])
    stats = jnp.stack([stats] + from_others(stats, "cent"))
    peak = jnp.max(stats[:, 0], axis=0)
    norm = jnp.sum(stats[:, 1] * jnp.exp(stats[:, 0] - peak[None, :]), axis=0)
    resp = (jnp.exp(logits - peak[None, :]) / norm[None, :]).astype(jnp.bfloat16)
    all_resp = lax.all_gather(resp, ("dp", "feat"), axis=0, tiled=False)
    features = [own_features] + [featurize(x, projection, phases) for x in others]
    order = [dp * n_feat + t for t in range(n_feat)] + [
        (dp + n_data - s) % n_data * n_feat + (feat + n_feat - t) % n_feat
        for s in range(1, n_data)
        for t in range(n_feat)
    ]
    order = jnp.stack(order).astype(jnp.int32)
    return update(order, all_resp, centroids, features, n_feat)


def solution(mesh):
    return jax.shard_map(
        shards,
        mesh=mesh,
        in_specs=(P(("dp", "cent"), None), P(None, "feat"), P("feat"), P("cent", "feat")),
        out_specs=P("cent", "feat"),
        check_vma=False,
    )
```

```python
import functools
import math

import jax
import jax.numpy as jnp
from jax import lax
from jax.experimental import pallas as pl
from jax.experimental.pallas import tpu as pltpu
from jax.sharding import PartitionSpec as P

F = 8192
SHARP_FACTOR = 1.5
PRIOR_MASS = 1.0

COS_COEFS = (
    1.4142135468471868,
    -0.7071066266011933,
    0.058925313538275806,
    -0.0019640317236862027,
    3.502984094725661e-05,
    -3.829489560381237e-07,
    2.4385896105334273e-09,
)
INV_TURN = 1.0 / (2.0 * math.pi)
TURN_COEFS = tuple(c * (2.0 * math.pi) ** (2 * k) for k, c in enumerate(COS_COEFS))


def scaled_cos(x):
    turns = x * INV_TURN
    r = turns - jnp.round(turns)
    u = r * r
    y = TURN_COEFS[-1]
    for c in TURN_COEFS[-2::-1]:
        y = y * u + c
    return y


def feature_kernel(sub_rows, sub_cols, e_ref, p_ref, b_ref, o_ref):
    rows, cols = o_ref.shape
    held = None
    for j in range(cols // sub_cols):
        cs = slice(j * sub_cols, (j + 1) * sub_cols)
        for i in range(rows // sub_rows):
            rs = slice(i * sub_rows, (i + 1) * sub_rows)
            x = jnp.dot(e_ref[rs, :], p_ref[:, cs], preferred_element_type=jnp.float32)
            if held is not None:
                hr, hc, hx = held
                o_ref[hr, hc] = scaled_cos(hx + b_ref[:, hc]).astype(jnp.bfloat16)
            held = rs, cs, x
    hr, hc, hx = held
    o_ref[hr, hc] = scaled_cos(hx + b_ref[:, hc]).astype(jnp.bfloat16)


def featurize(embeddings, projection, phases, total_rows, first_row, held):
    rows, width = embeddings.shape
    cols = projection.shape[1]
    tr, tc = min(1024, rows), min(1024, cols)
    first = first_row // tr
    kernel = functools.partial(feature_kernel, min(128, tr), min(256, tc))
    in_specs = [
        pl.BlockSpec((tr, width), lambda j, i: (i, 0)),
        pl.BlockSpec((width, tc), lambda j, i: (0, j)),
        pl.BlockSpec((1, tc), lambda j, i: (0, j)),
    ]
    operands = [embeddings, projection, phases.reshape(1, cols)]
    aliases = {}
    if held is not None:
        in_specs.append(pl.BlockSpec(memory_space=pl.ANY))
        operands.append(held)
        aliases = {3: 0}
    return pl.pallas_call(
        lambda *refs: kernel(*refs[:3], refs[-1]),
        grid=(cols // tc, rows // tr),
        in_specs=in_specs,
        out_specs=pl.BlockSpec((tr, tc), lambda j, i: (first + i, j)),
        out_shape=jax.ShapeDtypeStruct((total_rows, cols), jnp.bfloat16),
        input_output_aliases=aliases,
        compiler_params=pltpu.CompilerParams(vmem_limit_bytes=44 << 20),
        cost_estimate=pl.CostEstimate(
            flops=6 * rows * width * cols,
            bytes_accessed=2 * (rows * cols + rows * width + width * cols),
            transcendentals=0,
        ),
        name="featurize",
    )(*operands)


def score_kernel(tile, c_ref, f_ref, s_ref, o_ref):
    cents = c_ref.shape[0]
    for i in range(cents // tile):
        rs = slice(i * tile, (i + 1) * tile)
        inner = lax.dot_general(
            c_ref[rs, :],
            f_ref[...],
            (((1,), (1,)), ((), ())),
            preferred_element_type=jnp.float32,
        )
        o_ref[0, rs, :] = 2.0 * inner - s_ref[rs, :]


def score(centroids, features, center_sq, rows, groups):
    cents, cols = centroids.shape
    size = rows // groups
    return pl.pallas_call(
        functools.partial(score_kernel, min(256, cents)),
        grid=(groups,),
        in_specs=[
            pl.BlockSpec((cents, cols), lambda g: (0, 0)),
            pl.BlockSpec((size, cols), lambda g: (g, 0)),
            pl.BlockSpec((cents, 1), lambda g: (0, 0)),
        ],
        out_specs=pl.BlockSpec((1, cents, size), lambda g: (g, 0, 0)),
        out_shape=jax.ShapeDtypeStruct((groups, cents, size), jnp.float32),
        compiler_params=pltpu.CompilerParams(vmem_limit_bytes=40 << 20),
        cost_estimate=pl.CostEstimate(
            flops=2 * rows * cents * cols,
            bytes_accessed=2 * (rows * cols + cents * cols) + 4 * rows * cents,
            transcendentals=0,
        ),
        name="score",
    )(centroids, features, center_sq)


def update_kernel(n_parts, i_ref, *refs):
    r_refs = refs[:n_parts]
    c_ref, f_ref, o_ref, k_ref, m_ref = refs[n_parts:]
    size = r_refs[0].shape[1]

    @pl.when(pl.program_id(0) == 0)
    def _():
        mass = jnp.zeros(m_ref.shape, jnp.float32)
        for g in range(n_parts):
            part = r_refs[g][...]
            k_ref[:, pl.ds(pl.multiple_of(i_ref[g] * size, size), size)] = part
            mass += jnp.sum(part.astype(jnp.float32), axis=1, keepdims=True)
        m_ref[...] = mass

    total = jnp.dot(k_ref[...], f_ref[...], preferred_element_type=jnp.float32)
    o_ref[...] = (total + PRIOR_MASS * c_ref[...].astype(jnp.float32)) / (
        m_ref[...] + PRIOR_MASS
    )


def update(places, resp_parts, centroids, features):
    cents, size = resp_parts[0].shape
    rows, cols = features.shape
    tc = min(512, cols)
    return pl.pallas_call(
        functools.partial(update_kernel, len(resp_parts)),
        grid=(cols // tc,),
        in_specs=[pl.BlockSpec(memory_space=pltpu.SMEM)]
        + [
            pl.BlockSpec((cents, size), lambda j: (0, 0), pipeline_mode=pl.Buffered(1))
            for _ in resp_parts
        ]
        + [
            pl.BlockSpec((cents, tc), lambda j: (0, j)),
            pl.BlockSpec((rows, tc), lambda j: (0, j)),
        ],
        out_specs=pl.BlockSpec((cents, tc), lambda j: (0, j)),
        out_shape=jax.ShapeDtypeStruct((cents, cols), jnp.float32),
        scratch_shapes=[
            pltpu.VMEM((cents, rows), jnp.bfloat16),
            pltpu.VMEM((cents, 1), jnp.float32),
        ],
        compiler_params=pltpu.CompilerParams(vmem_limit_bytes=52 << 20),
        cost_estimate=pl.CostEstimate(
            flops=2 * rows * cents * cols,
            bytes_accessed=2 * (rows * cols + rows * cents) + 6 * cents * cols,
            transcendentals=0,
        ),
        name="update",
    )(places, *resp_parts, centroids, features)


def my_part(x, axis_name):
    size = x.shape[0] // lax.axis_size(axis_name)
    return lax.dynamic_slice_in_dim(x, lax.axis_index(axis_name) * size, size, 0)


def from_others(x, axis_name):
    n = lax.axis_size(axis_name)
    return [
        lax.ppermute(x, axis_name, [(i, (i + s) % n) for i in range(n)]) for s in range(1, n)
    ]


def shards(embeddings, projection, phases, centroids):
    sharpness = SHARP_FACTOR / math.sqrt(F)
    n_data, n_feat = lax.axis_size("dp"), lax.axis_size("feat")
    dp, feat = lax.axis_index("dp"), lax.axis_index("feat")
    own = lax.all_gather(my_part(embeddings, "feat"), ("cent", "feat"), axis=0, tiled=True)
    halves = from_others(my_part(own, "feat"), "dp")
    wide = centroids.astype(jnp.float32)
    center_sq = jnp.sum(wide * wide, axis=1, keepdims=True)
    depth = own.shape[0]
    total_rows = depth * n_data
    features = featurize(own, projection, phases, total_rows, 0, None)
    partial_value = score(centroids, features, center_sq, depth, n_feat)
    partial_value, *halves = lax.optimization_barrier((partial_value, *halves))
    others = [
        jnp.concatenate([half] + from_others(half, "feat"), axis=0) for half in halves
    ]
    whole_value = lax.psum_scatter(partial_value, "feat", scatter_dimension=0)
    whole_value, *others = lax.optimization_barrier((whole_value, *others))
    logits = sharpness * whole_value
    top = jnp.max(logits, axis=0)
    local_sum = jnp.sum(jnp.exp(logits - top[None, :]), axis=0)
    stats = jnp.stack([top, local_sum])
    stats = jnp.stack([stats] + from_others(stats, "cent"))
    peak = jnp.max(stats[:, 0], axis=0)
    norm = jnp.sum(stats[:, 1] * jnp.exp(stats[:, 0] - peak[None, :]), axis=0)
    resp = (jnp.exp(logits - peak[None, :]) / norm[None, :]).astype(jnp.bfloat16)
    parts = [resp] + from_others(resp, "feat")
    far = from_others(resp, "dp")
    for s in range(1, n_data - 1):
        features = featurize(others[s - 1], projection, phases, total_rows, s * depth, features)
    features, *far = lax.optimization_barrier((features, *far))
    for part in far:
        parts += [part] + from_others(part, "feat")
    s = n_data - 1
    features = featurize(others[s - 1], projection, phases, total_rows, s * depth, features)
    places = [(feat + n_feat - t) % n_feat for t in range(n_feat)]
    places += [feat * 0 + g for g in range(n_feat, n_data * n_feat)]
    places = jnp.stack(places).astype(jnp.int32)
    return update(places, parts, centroids, features)


def solution(mesh):
    return jax.shard_map(
        shards,
        mesh=mesh,
        in_specs=(P(("dp", "cent"), None), P(None, "feat"), P("feat"), P("cent", "feat")),
        out_specs=P("cent", "feat"),
        check_vma=False,
    )
```
